32 devices in a mesh: dp: 4 (over y, x), tensor: 8 (over z, core).
Axes of the slice: x: 2, y: 2, z: 4, core: 2. Of those that a mesh axis runs over, the one named last changes fastest.
Arguments:
- tokens: bfloat16 [2048, 8192], P(('dp', 'tensor')), may hold values from -6 to 6
- w_query: bfloat16 [8192, 8192], P(None, 'tensor'), may hold values from -0.0625 to 0.0625
- cotangent: bfloat16 [2048, 8192], P('dp', 'tensor'), may hold values from -6 to 6
- task_embed: bfloat16 [128, 1024], replicated, may hold values from -6 to 6
- w_hidden: bfloat16 [1024, 512], P(None, 'tensor'), may hold values from -0.1875 to 0.1875
- head_a: bfloat16 [512, 16, 8192], P(None, 'dp', 'tensor'), may hold values from -0.0234375 to 0.0234375
- head_b: bfloat16 [512, 16, 8192], P(None, 'dp', 'tensor'), may hold values from -0.0234375 to 0.0234375
- block_task: int32 [4], replicated, may hold values from 0 to 127
Outputs:
- output: bfloat16 [2048, 8192], P('dp', 'tensor')
- grad_tokens: bfloat16 [2048, 8192], P(('dp', 'tensor'))
- grad_head_a: bfloat16 [512, 16, 8192], P(None, 'dp', 'tensor')
- grad_head_b: bfloat16 [512, 16, 8192], P(None, 'dp', 'tensor')
The draws below stay inside these ranges and needn't reach their ends.
All inputs are finite; a program needn't handle non-finite values.
Results may differ from the reference program's by a relative error of at most 0.0077.
Values may be sent and summed in bfloat16 or wider, within the bound.
A program may use at most 128 MiB of HBM per device.

```python
import math
import jax
import jax.numpy as jnp
import numpy as np
from jax import lax

MODEL_DIM = 8192
R = 16
HID = 512
EMB = 1024
NTASK = 128
BLOCK_TOKENS = 512
NBLK = 4
TOTAL_TOKENS = 2048


def touch_ends(array, own_key, smallest, top_value):
    longest = array.shape.index(max(array.shape))
    spots = []
    for shift in (0, 1):
        where = [jax.random.randint(jax.random.fold_in(own_key, axis), (), 0, length) for axis, length in enumerate(array.shape)]
        where[longest] = (where[longest] + shift) % array.shape[longest]
        spots.append(tuple(where))
    return array.at[spots[0]].set(smallest).at[spots[1]].set(top_value)


def levels(stream_key, dims, shards, least, largest):
    level, own = 1.0, jax.random.fold_in(stream_key, 6)
    for position, parts in shards:
        draws = jnp.exp(jax.random.uniform(jax.random.fold_in(own, position), (parts,), jnp.float32, least / len(shards), largest / len(shards)))
        level = level * jnp.repeat(draws, dims[position] // parts).reshape([-1 if axis == position else 1 for axis in range(len(dims))])
    return level


def rank_table(count, skew):
    portions = [(1 << 20) // math.isqrt(grade ** skew) + 1 for grade in range(1, count + 1)]
    scale = 1 + sum(portions) // (1 << 30)
    return np.cumsum(np.array([max(1, weight // scale) for weight in portions]))


def ranked_ids(key, dims, count, lean):
    table = rank_table(count, lean)
    pick = jax.random.randint(jax.random.fold_in(key, 1), dims, 0, int(table[count - 1]))
    rank = jnp.searchsorted(jnp.asarray(table, jnp.int32), pick, side="right")
    return jax.random.permutation(jax.random.fold_in(key, 2), count)[rank].astype(jnp.int32)


def normal_values(key, dims, deviation, reach, split=(), kind=jnp.bfloat16):
    result = deviation * jax.random.normal(key, dims, jnp.float32)
    if split:
        result = result * levels(key, dims, split, -0.22, 0.18)
    return jnp.clip(result, -reach, reach).astype(kind)


def setup_inputs(seed: int = 0) -> dict:
    seeds = jax.random.split(jax.random.key(seed), 9)
    tokens = normal_values(seeds[0], (TOTAL_TOKENS, MODEL_DIM), 1.0, 6.0, ((0, 32),))
    w_query = normal_values(seeds[1], (MODEL_DIM, MODEL_DIM), MODEL_DIM ** -0.5, 0.0625, ((1, 8),))
    cotangent = normal_values(seeds[2], (TOTAL_TOKENS, MODEL_DIM), 1.0, 6.0, ((0, 4), (1, 8)))
    task_embed = normal_values(seeds[3], (NTASK, EMB), 1.0, 6.0)
    w_hidden = normal_values(seeds[4], (EMB, HID), EMB ** -0.5, 0.1875, ((1, 8),))
    head_a = normal_values(seeds[5], (HID, R, MODEL_DIM), (HID * 128) ** -0.5, 0.0234375, ((1, 4), (2, 8)))
    head_b = normal_values(seeds[6], (HID, R, MODEL_DIM), (HID * 128) ** -0.5, 0.0234375, ((1, 4), (2, 8)))
    block_task = touch_ends(ranked_ids(seeds[7], (NBLK,), NTASK, 2), jax.random.fold_in(seeds[7], 3), 0, NTASK - 1).astype(jnp.int32)
    return {"tokens": tokens, "w_query": w_query, "cotangent": cotangent, "task_embed": task_embed, "w_hidden": w_hidden, "head_a": head_a, "head_b": head_b, "block_task": block_task}


def reference(tokens, w_query, cotangent, task_embed, w_hidden, head_a, head_b, block_task):
    single_float = jnp.float32
    brain_half_float = jnp.bfloat16
    hidden = jax.nn.silu(jnp.dot(task_embed, w_hidden, preferred_element_type=single_float)).astype(brain_half_float)
    hid_blocks = hidden[block_task]
    adapter_down_weight = jnp.dot(hid_blocks, head_a.reshape(HID, R * MODEL_DIM), preferred_element_type=single_float).astype(brain_half_float).reshape(NBLK, R, MODEL_DIM)
    adapter_up_weight = jnp.dot(hid_blocks, head_b.reshape(HID, R * MODEL_DIM), preferred_element_type=single_float).astype(brain_half_float).reshape(NBLK, R, MODEL_DIM)
    block_inputs = tokens.reshape(NBLK, BLOCK_TOKENS, MODEL_DIM).astype(single_float)
    block_output_grads = cotangent.reshape(NBLK, BLOCK_TOKENS, MODEL_DIM).astype(single_float)
    frozen_output = jnp.dot(tokens, w_query, preferred_element_type=single_float)
    down_projection = jnp.einsum("grs,gps->grp", block_inputs, adapter_down_weight.astype(single_float))
    down_low_rank = down_projection.astype(brain_half_float)
    low_rank_update = jnp.einsum("elm,emn->eln", down_low_rank.astype(single_float), adapter_up_weight.astype(single_float)).reshape(TOTAL_TOKENS, MODEL_DIM)
    output = (frozen_output + low_rank_update).astype(brain_half_float)
    backward_input = jnp.einsum("grs,gps->grp", block_output_grads, adapter_up_weight.astype(single_float))
    backward_low_rank = backward_input.astype(brain_half_float)
    frozen = lax.dot_general(cotangent, w_query, (((1,), (1,)), ((), ())), preferred_element_type=single_float)
    adapter_output = jnp.einsum("elm,emn->eln", backward_low_rank.astype(single_float), adapter_down_weight.astype(single_float)).reshape(TOTAL_TOKENS, MODEL_DIM)
    grad_tokens = (frozen + adapter_output).astype(brain_half_float)
    adapter_down_gradient = (jnp.einsum("evr,evx->erx", backward_low_rank.astype(single_float), block_inputs) / BLOCK_TOKENS).astype(brain_half_float)
    adapter_up_gradient = (jnp.einsum("evr,evx->erx", down_low_rank.astype(single_float), block_output_grads) / BLOCK_TOKENS).astype(brain_half_float)
    hid_f = hid_blocks.astype(single_float)
    grad_head_a = lax.dot_general(hid_f, adapter_down_gradient.astype(single_float).reshape(NBLK, R * MODEL_DIM), (((0,), (0,)), ((), ())), precision=lax.Precision.HIGHEST)
    grad_head_b = lax.dot_general(hid_f, adapter_up_gradient.astype(single_float).reshape(NBLK, R * MODEL_DIM), (((0,), (0,)), ((), ())), precision=lax.Precision.HIGHEST)
    return (output, grad_tokens, grad_head_a.reshape(HID, R, MODEL_DIM).astype(brain_half_float), grad_head_b.reshape(HID, R, MODEL_DIM).astype(brain_half_float))
```

```python
import functools

import jax
import jax.numpy as jnp
from jax import lax
from jax.experimental import pallas as pl
from jax.experimental.pallas import tpu as pltpu
from jax.sharding import PartitionSpec as P

F32 = jnp.float32
BF16 = jnp.bfloat16
MESH = pl.DeviceIdType.MESH
GRAD_CHUNKS = 8
SKEW = 2


def exchange_kernel(axis, n, scatter, x_ref, out_ref, send_sem, recv_sem):
    me = lax.axis_index(axis)
    barrier = pltpu.get_barrier_semaphore()
    for k in range(1, n):
        pl.semaphore_signal(
            barrier, inc=1, device_id={axis: lax.rem(me + k, n)}, device_id_type=MESH
        )
    pl.semaphore_wait(barrier, n - 1)
    copies = []
    for k in range(1, n):
        target = lax.rem(me + k, n)
        copy = pltpu.make_async_remote_copy(
            src_ref=x_ref.at[target] if scatter else x_ref,
            dst_ref=out_ref.at[me],
            send_sem=send_sem.at[k],
            recv_sem=recv_sem.at[k],
            device_id={axis: target},
            device_id_type=MESH,
        )
        copy.start()
        copies.append(copy)
    out_ref[me] = x_ref[me] if scatter else x_ref[...]
    for copy in copies:
        copy.wait()


def exchange(x, axis, n, scatter, cid):
    rows, lanes = x.shape[-2:]
    x = x.astype(F32)
    x = jnp.pad(x, [(0, 0)] * (x.ndim - 2) + [(0, -rows % 8), (0, -lanes % 128)])
    shape = x.shape if scatter else (n,) + x.shape
    got = pl.pallas_call(
        functools.partial(exchange_kernel, axis, n, scatter),
        out_shape=jax.ShapeDtypeStruct(shape, x.dtype),
        in_specs=[pl.BlockSpec(memory_space=pltpu.VMEM)],
        out_specs=pl.BlockSpec(memory_space=pltpu.VMEM),
        scratch_shapes=[pltpu.SemaphoreType.DMA((n,)), pltpu.SemaphoreType.DMA((n,))],
        compiler_params=pltpu.CompilerParams(collective_id=cid, has_side_effects=True),
    )(x)
    return got[..., :rows, :lanes]


def gradient_kernel(n, chunks, g_ref, w_ref, out_ref, w_buf, mine, give, theirs, up_out, up_in, down_out, down_in,
                    w_sem, pair_send, pair_recv, up_send, up_recv, down_send, down_recv):
    shard = lax.axis_index("tensor")
    z, core = shard // 2, lax.rem(shard, 2)
    chips = n // 2
    steps = chips - 1
    rows = out_ref.shape[0]
    cw = w_buf.shape[1]
    pair = {"tensor": 2 * z + 1 - core}
    above = {"tensor": lax.rem(shard + 2, n)}
    below = {"tensor": lax.rem(shard + n - 2, n)}
    has_above, has_below = z < chips - 1, z > 0

    barrier = pltpu.get_barrier_semaphore()
    pl.semaphore_signal(barrier, inc=1, device_id=pair, device_id_type=MESH)

    @pl.when(has_above)
    def _():
        pl.semaphore_signal(barrier, inc=1, device_id=above, device_id_type=MESH)

    @pl.when(has_below)
    def _():
        pl.semaphore_signal(barrier, inc=1, device_id=below, device_id_type=MESH)

    def fetch(c):
        slot = lax.rem(c, 2)
        return pltpu.make_async_copy(
            w_ref.at[pl.ds(pl.multiple_of(c * cw, cw), cw)], w_buf.at[slot], w_sem.at[slot]
        )

    fetch(0).start()
    pl.semaphore_wait(
        barrier, 1 + jnp.where(has_above, 1, 0) + jnp.where(has_below, 1, 0)
    )

    def pair_copy(c):
        return pltpu.make_async_remote_copy(
            src_ref=give.at[c],
            dst_ref=theirs.at[c],
            send_sem=pair_send.at[c],
            recv_sem=pair_recv.at[c],
            device_id=pair,
            device_id_type=MESH,
        )

    def up_copy(c, s):
        return pltpu.make_async_remote_copy(
            src_ref=up_out.at[c, s],
            dst_ref=up_in.at[c, s],
            send_sem=up_send.at[c, s],
            recv_sem=up_recv.at[c, s],
            device_id=above,
            device_id_type=MESH,
        )

    def down_copy(c, s):
        return pltpu.make_async_remote_copy(
            src_ref=down_out.at[c, s],
            dst_ref=down_in.at[c, s],
            send_sem=down_send.at[c, s],
            recv_sem=down_recv.at[c, s],
            device_id=below,
            device_id_type=MESH,
        )

    def product(i, w):
        return lax.dot_general(
            g_ref[i], w, (((1,), (1,)), ((), ())), preferred_element_type=F32
        ).astype(BF16).reshape(chips, rows, cw)

    def multiply(c):
        @pl.when(c + 1 < chunks)
        def _():
            fetch(c + 1).start()

        fetch(c).wait()
        w = w_buf[lax.rem(c, 2)]
        give[c] = product(0, w)
        pair_copy(c).start()
        mine[c] = product(1, w)

    def both(c, d):
        return mine[c, d].astype(F32) + theirs[c, d].astype(F32)

    def forward(c, s):
        if s == 0:
            pair_copy(c).wait_recv()
        far = steps - s

        @pl.when(z <= s)
        def _():
            total = both(c, z + far)
            if s == 0:
                up_out[c, s] = total.astype(BF16)
            else:
                @pl.when(has_below)
                def _():
                    up_copy(c, s - 1).wait_recv()
                    up_out[c, s] = (total + up_in[c, s - 1].astype(F32)).astype(BF16)

                @pl.when(jnp.logical_not(has_below))
                def _():
                    up_out[c, s] = total.astype(BF16)
            up_copy(c, s).start()

        @pl.when(z >= far)
        def _():
            total = both(c, z - far)
            if s == 0:
                down_out[c, s] = total.astype(BF16)
            else:
                @pl.when(has_above)
                def _():
                    down_copy(c, s - 1).wait_recv()
                    down_out[c, s] = (total + down_in[c, s - 1].astype(F32)).astype(BF16)

                @pl.when(jnp.logical_not(has_above))
                def _():
                    down_out[c, s] = total.astype(BF16)
            down_copy(c, s).start()

    def finish(c):
        columns = pl.ds(pl.multiple_of(c * cw, cw), cw)
        if steps == 0:
            pair_copy(c).wait_recv()
        out_ref[:, columns] = both(c, z)
        if steps:
            @pl.when(has_below)
            def _():
                up_copy(c, steps - 1).wait_recv()
                out_ref[:, columns] += up_in[c, steps - 1].astype(F32)

            @pl.when(has_above)
            def _():
                down_copy(c, steps - 1).wait_recv()
                out_ref[:, columns] += down_in[c, steps - 1].astype(F32)

    def at(c, stage):
        @pl.when(jnp.logical_and(c >= 0, c < chunks))
        def _():
            stage(c)

    def turn(t, carry):
        at(t, multiply)
        for s in range(steps):
            at(t - 1 - SKEW * s, lambda c, s=s: forward(c, s))
        at(t - 1 - SKEW * steps, finish)
        return carry

    lax.fori_loop(0, chunks + 1 + SKEW * steps, turn, 0)

    def settle(c, carry):
        pair_copy(c).wait_send()
        for s in range(steps):
            @pl.when(z <= s)
            def _(s=s):
                up_copy(c, s).wait_send()

            @pl.when(z >= steps - s)
            def _(s=s):
                down_copy(c, s).wait_send()
        return carry

    lax.fori_loop(0, chunks, settle, 0)


def summed_gradient(grads, w, n, rows, cid):
    chips = n // 2
    model_width, width = w.shape
    cw = model_width // GRAD_CHUNKS
    steps = max(chips - 1, 1)
    all_rows = pltpu.VMEM((GRAD_CHUNKS, chips, rows, cw), BF16)
    hops = pltpu.VMEM((GRAD_CHUNKS, steps, rows, cw), BF16)
    pair_sem = pltpu.SemaphoreType.DMA((GRAD_CHUNKS,))
    hop_sem = pltpu.SemaphoreType.DMA((GRAD_CHUNKS, steps))
    vmem = pl.BlockSpec(memory_space=pltpu.VMEM)
    return pl.pallas_call(
        functools.partial(gradient_kernel, n, GRAD_CHUNKS),
        out_shape=jax.ShapeDtypeStruct((rows, model_width), F32),
        in_specs=[vmem, pl.BlockSpec(memory_space=pl.ANY)],
        out_specs=vmem,
        scratch_shapes=[pltpu.VMEM((2, cw, width), BF16)]
        + [all_rows] * 3
        + [hops] * 4
        + [pltpu.SemaphoreType.DMA((2,))]
        + [pair_sem] * 2
        + [hop_sem] * 4,
        compiler_params=pltpu.CompilerParams(
            collective_id=cid, has_side_effects=True, vmem_limit_bytes=48 * 1024 * 1024
        ),
        cost_estimate=pl.CostEstimate(
            flops=2 * rows * n * model_width * width,
            bytes_accessed=model_width * width * 12,
            transcendentals=0,
        ),
    )(grads, w)


def local(tokens, w_query, cotangent, task_embed, w_hidden, head_a, head_b, block_task):
    n_groups = lax.axis_size("dp")
    n_shards = lax.axis_size("tensor")
    chips = n_shards // 2
    shard = lax.axis_index("tensor")
    z, core = shard // 2, shard % 2
    hid_count, rank_rows, width = head_a.shape
    rank = rank_rows * n_groups
    blocks = block_task.shape[0]
    per_group = blocks // n_groups
    rows_dev, model_width = tokens.shape
    rows_all = rows_dev * n_shards
    block = rows_all // per_group

    whole = lax.all_gather(tokens, "tensor", axis=0, tiled=True)

    by_core = cotangent.reshape(chips, 2, rows_dev, width)
    by_core = jnp.where(core == 0, by_core[:, ::-1], by_core)
    by_core = jnp.swapaxes(by_core, 0, 1).reshape(2, chips * rows_dev, width)
    frozen = summed_gradient(by_core, w_query, n_shards, rows_dev, 6)

    part = jax.nn.silu(
        jnp.dot(task_embed[block_task], w_hidden, preferred_element_type=F32)
    ).astype(BF16)
    hidden = exchange(part.astype(F32), "tensor", n_shards, False, 0)
    hidden = jnp.swapaxes(hidden, 0, 1).reshape(blocks, hid_count).astype(BF16)

    def generate(head):
        made = jnp.dot(
            hidden, head.reshape(hid_count, rank_rows * width), preferred_element_type=F32
        )
        return made.astype(BF16).astype(F32).reshape(n_groups, per_group, rank_rows, width)

    made = jnp.stack([generate(head_a), generate(head_b)], 1)
    made = made.reshape(n_groups, 2 * per_group * rank_rows, width)
    made = exchange(made, "dp", n_groups, True, 1).astype(BF16)
    made = made.reshape(n_groups, 2, per_group, rank_rows, width)
    made = made.transpose(1, 2, 0, 3, 4).reshape(2, per_group, rank, width)
    down_weight, up_weight = made[0], made[1]
    full_a = exchange(down_weight.reshape(per_group * rank, width), "tensor", n_shards, False, 2).astype(BF16)
    full_a = jnp.swapaxes(full_a, 0, 1).reshape(per_group, rank, model_width)
    which = shard * rows_dev // block
    a_here = lax.dynamic_index_in_dim(full_a, which, 0, keepdims=False)

    grads_in = cotangent.reshape(per_group, block, width)
    back_part = jnp.einsum("gps,grs->pgr", up_weight, grads_in, preferred_element_type=F32)
    down_own = jnp.einsum("ps,rs->pr", a_here, tokens, preferred_element_type=F32)
    both_parts = jnp.concatenate([back_part.reshape(rank, rows_all), down_own], 1)
    both_parts = exchange(both_parts, "tensor", n_shards, False, 3)
    back_low = both_parts[:, :, :rows_all].sum(0).astype(BF16)
    down_low = jnp.swapaxes(both_parts[:, :, rows_all:], 0, 1).reshape(rank, rows_all).astype(BF16)

    base = jnp.dot(whole, w_query, preferred_element_type=F32)
    update = jnp.einsum(
        "pgr,gpn->grn",
        down_low.reshape(rank, per_group, block),
        up_weight,
        preferred_element_type=F32,
    ).reshape(rows_all, width)
    output = (base + update).astype(BF16)

    back_here = lax.dynamic_slice_in_dim(back_low, shard * rows_dev, rows_dev, 1)
    grad_tokens = (
        frozen
        + jnp.einsum("pr,pd->rd", back_here, a_here, preferred_element_type=F32)
    ).astype(BF16)

    scale = 1.0 / block
    columns = lax.dynamic_slice_in_dim(whole, shard * width, width, 1)
    grad_a = jnp.einsum(
        "pgr,grd->pgd",
        back_low.reshape(rank, per_group, block),
        columns.reshape(per_group, block, width),
        preferred_element_type=F32,
    )
    grad_b = jnp.einsum(
        "pgr,grd->pgd",
        down_low.reshape(rank, per_group, block),
        grads_in,
        preferred_element_type=F32,
    )

    def send_back(grad, cid):
        low = (grad * scale).astype(BF16).astype(F32)
        low = low.reshape(n_groups, rank_rows * per_group, width)
        got = exchange(low, "dp", n_groups, True, cid)
        got = got.reshape(n_groups, rank_rows, per_group, width)
        return jnp.swapaxes(got, 1, 2).reshape(blocks, rank_rows, width)

    hid_f = hidden.astype(F32)

    def head_grad(got):
        return sum(
            hid_f[b][:, None, None] * got[b][None] for b in range(blocks)
        ).astype(BF16)

    grad_head_b = head_grad(send_back(grad_b, 4))
    grad_head_a = head_grad(send_back(grad_a, 5))
    return (output, grad_tokens, grad_head_a, grad_head_b)


def solution(mesh):
    return jax.shard_map(
        local,
        mesh=mesh,
        in_specs=(
            P(("dp", "tensor"), None),
            P(None, "tensor"),
            P("dp", "tensor"),
            P(),
            P(None, "tensor"),
            P(None, "dp", "tensor"),
            P(None, "dp", "tensor"),
            P(),
        ),
        out_specs=(
            P("dp", "tensor"),
            P(("dp", "tensor"), None),
            P(None, "dp", "tensor"),
            P(None, "dp", "tensor"),
        ),
        check_vma=False,
    )
```

```python
import functools

import jax
import jax.numpy as jnp
from jax import lax
from jax.experimental import pallas as pl
from jax.experimental.pallas import tpu as pltpu
from jax.sharding import PartitionSpec as P

F32 = jnp.float32
BF16 = jnp.bfloat16
MESH = pl.DeviceIdType.MESH
GRAD_CHUNKS = 8
SKEW = 2


def exchange_kernel(axis, n, scatter, x_ref, out_ref, send_sem, recv_sem):
    me = lax.axis_index(axis)
    barrier = pltpu.get_barrier_semaphore()
    for k in range(1, n):
        pl.semaphore_signal(
            barrier, inc=1, device_id={axis: lax.rem(me + k, n)}, device_id_type=MESH
        )
    pl.semaphore_wait(barrier, n - 1)
    copies = []
    for k in range(1, n):
        target = lax.rem(me + k, n)
        copy = pltpu.make_async_remote_copy(
            src_ref=x_ref.at[target] if scatter else x_ref,
            dst_ref=out_ref.at[me],
            send_sem=send_sem.at[k],
            recv_sem=recv_sem.at[k],
            device_id={axis: target},
            device_id_type=MESH,
        )
        copy.start()
        copies.append(copy)
    out_ref[me] = x_ref[me] if scatter else x_ref[...]
    for copy in copies:
        copy.wait()


def exchange(x, axis, n, scatter, cid):
    rows, lanes = x.shape[-2:]
    x = x.astype(F32)
    x = jnp.pad(x, [(0, 0)] * (x.ndim - 2) + [(0, -rows % 8), (0, -lanes % 128)])
    shape = x.shape if scatter else (n,) + x.shape
    got = pl.pallas_call(
        functools.partial(exchange_kernel, axis, n, scatter),
        out_shape=jax.ShapeDtypeStruct(shape, x.dtype),
        in_specs=[pl.BlockSpec(memory_space=pltpu.VMEM)],
        out_specs=pl.BlockSpec(memory_space=pltpu.VMEM),
        scratch_shapes=[pltpu.SemaphoreType.DMA((n,)), pltpu.SemaphoreType.DMA((n,))],
        compiler_params=pltpu.CompilerParams(collective_id=cid, has_side_effects=True),
    )(x)
    return got[..., :rows, :lanes]


def gradient_kernel(n, chunks, g_ref, w_ref, out_ref, w_buf, mine, give, theirs, up_out, up_in, down_out, down_in,
                    w_sem, pair_send, pair_recv, up_send, up_recv, down_send, down_recv):
    shard = lax.axis_index("tensor")
    z, core = shard // 2, lax.rem(shard, 2)
    chips = n // 2
    steps = chips - 1
    rows = out_ref.shape[0]
    cw = w_buf.shape[1]
    pair = {"tensor": 2 * z + 1 - core}
    above = {"tensor": lax.rem(shard + 2, n)}
    below = {"tensor": lax.rem(shard + n - 2, n)}
    has_above, has_below = z < chips - 1, z > 0

    barrier = pltpu.get_barrier_semaphore()
    pl.semaphore_signal(barrier, inc=1, device_id=pair, device_id_type=MESH)

    @pl.when(has_above)
    def _():
        pl.semaphore_signal(barrier, inc=1, device_id=above, device_id_type=MESH)

    @pl.when(has_below)
    def _():
        pl.semaphore_signal(barrier, inc=1, device_id=below, device_id_type=MESH)

    def fetch(c):
        slot = lax.rem(c, 2)
        return pltpu.make_async_copy(
            w_ref.at[pl.ds(pl.multiple_of(c * cw, cw), cw)], w_buf.at[slot], w_sem.at[slot]
        )

    fetch(0).start()
    pl.semaphore_wait(
        barrier, 1 + jnp.where(has_above, 1, 0) + jnp.where(has_below, 1, 0)
    )

    def pair_copy(c):
        return pltpu.make_async_remote_copy(
            src_ref=give.at[c],
            dst_ref=theirs.at[c],
            send_sem=pair_send.at[c],
            recv_sem=pair_recv.at[c],
            device_id=pair,
            device_id_type=MESH,
        )

    def up_copy(c, s):
        return pltpu.make_async_remote_copy(
            src_ref=up_out.at[c, s],
            dst_ref=up_in.at[c, s],
            send_sem=up_send.at[c, s],
            recv_sem=up_recv.at[c, s],
            device_id=above,
            device_id_type=MESH,
        )

    def down_copy(c, s):
        return pltpu.make_async_remote_copy(
            src_ref=down_out.at[c, s],
            dst_ref=down_in.at[c, s],
            send_sem=down_send.at[c, s],
            recv_sem=down_recv.at[c, s],
            device_id=below,
            device_id_type=MESH,
        )

    def product(i, w):
        return lax.dot_general(
            g_ref[i], w, (((1,), (1,)), ((), ())), preferred_element_type=F32
        ).astype(BF16).reshape(chips, rows, cw)

    def multiply(c):
        @pl.when(c + 1 < chunks)
        def _():
            fetch(c + 1).start()

        fetch(c).wait()
        w = w_buf[lax.rem(c, 2)]
        give[c] = product(0, w)
        pair_copy(c).start()
        mine[c] = product(1, w)

    def both(c, d):
        return mine[c, d].astype(F32) + theirs[c, d].astype(F32)

    def forward(c, s):
        if s == 0:
            pair_copy(c).wait_recv()
        far = steps - s

        @pl.when(z <= s)
        def _():
            total = both(c, z + far)
            if s == 0:
                up_out[c, s] = total.astype(BF16)
            else:
                @pl.when(has_below)
                def _():
                    up_copy(c, s - 1).wait_recv()
                    up_out[c, s] = (total + up_in[c, s - 1].astype(F32)).astype(BF16)

                @pl.when(jnp.logical_not(has_below))
                def _():
                    up_out[c, s] = total.astype(BF16)
            up_copy(c, s).start()

        @pl.when(z >= far)
        def _():
            total = both(c, z - far)
            if s == 0:
                down_out[c, s] = total.astype(BF16)
            else:
                @pl.when(has_above)
                def _():
                    down_copy(c, s - 1).wait_recv()
                    down_out[c, s] = (total + down_in[c, s - 1].astype(F32)).astype(BF16)

                @pl.when(jnp.logical_not(has_above))
                def _():
                    down_out[c, s] = total.astype(BF16)
            down_copy(c, s).start()

    def finish(c):
        columns = pl.ds(pl.multiple_of(c * cw, cw), cw)
        if steps == 0:
            pair_copy(c).wait_recv()
        out_ref[:, columns] = both(c, z)
        if steps:
            @pl.when(has_below)
            def _():
                up_copy(c, steps - 1).wait_recv()
                out_ref[:, columns] += up_in[c, steps - 1].astype(F32)

            @pl.when(has_above)
            def _():
                down_copy(c, steps - 1).wait_recv()
                out_ref[:, columns] += down_in[c, steps - 1].astype(F32)

    def at(c, stage):
        @pl.when(jnp.logical_and(c >= 0, c < chunks))
        def _():
            stage(c)

    def turn(t, carry):
        at(t, multiply)
        for s in range(steps):
            at(t - 1 - SKEW * s, lambda c, s=s: forward(c, s))
        at(t - 1 - SKEW * steps, finish)
        return carry

    lax.fori_loop(0, chunks + 1 + SKEW * steps, turn, 0)

    def settle(c, carry):
        pair_copy(c).wait_send()
        for s in range(steps):
            @pl.when(z <= s)
            def _(s=s):
                up_copy(c, s).wait_send()

            @pl.when(z >= steps - s)
            def _(s=s):
                down_copy(c, s).wait_send()
        return carry

    lax.fori_loop(0, chunks, settle, 0)


def summed_gradient(grads, w, n, rows, cid):
    chips = n // 2
    model_width, width = w.shape
    cw = model_width // GRAD_CHUNKS
    steps = max(chips - 1, 1)
    all_rows = pltpu.VMEM((GRAD_CHUNKS, chips, rows, cw), BF16)
    hops = pltpu.VMEM((GRAD_CHUNKS, steps, rows, cw), BF16)
    pair_sem = pltpu.SemaphoreType.DMA((GRAD_CHUNKS,))
    hop_sem = pltpu.SemaphoreType.DMA((GRAD_CHUNKS, steps))
    vmem = pl.BlockSpec(memory_space=pltpu.VMEM)
    return pl.pallas_call(
        functools.partial(gradient_kernel, n, GRAD_CHUNKS),
        out_shape=jax.ShapeDtypeStruct((rows, model_width), F32),
        in_specs=[vmem, pl.BlockSpec(memory_space=pl.ANY)],
        out_specs=vmem,
        scratch_shapes=[pltpu.VMEM((2, cw, width), BF16)]
        + [all_rows] * 3
        + [hops] * 4
        + [pltpu.SemaphoreType.DMA((2,))]
        + [pair_sem] * 2
        + [hop_sem] * 4,
        compiler_params=pltpu.CompilerParams(
            collective_id=cid, has_side_effects=True, vmem_limit_bytes=48 * 1024 * 1024
        ),
        cost_estimate=pl.CostEstimate(
            flops=2 * rows * n * model_width * width,
            bytes_accessed=model_width * width * 12,
            transcendentals=0,
        ),
    )(grads, w)


def local(tokens, w_query, cotangent, task_embed, w_hidden, head_a, head_b, block_task):
    n_groups = lax.axis_size("dp")
    n_shards = lax.axis_size("tensor")
    chips = n_shards // 2
    shard = lax.axis_index("tensor")
    z, core = shard // 2, shard % 2
    hid_count, rank_rows, width = head_a.shape
    rank = rank_rows * n_groups
    blocks = block_task.shape[0]
    per_group = blocks // n_groups
    rows_dev, model_width = tokens.shape
    rows_all = rows_dev * n_shards
    block = rows_all // per_group

    whole = lax.all_gather(tokens, "tensor", axis=0, tiled=True)

    by_core = cotangent.reshape(chips, 2, rows_dev, width)
    by_core = jnp.where(core == 0, by_core[:, ::-1], by_core)
    by_core = jnp.swapaxes(by_core, 0, 1).reshape(2, chips * rows_dev, width)
    frozen = summed_gradient(by_core, w_query, n_shards, rows_dev, 6)
    frozen, task_embed = lax.optimization_barrier((frozen, task_embed))

    part = jax.nn.silu(
        jnp.dot(task_embed[block_task], w_hidden, preferred_element_type=F32)
    ).astype(BF16)
    hidden = exchange(part.astype(F32), "tensor", n_shards, False, 0)
    hidden = jnp.swapaxes(hidden, 0, 1).reshape(blocks, hid_count).astype(BF16)

    def generate(head):
        made = jnp.dot(
            hidden, head.reshape(hid_count, rank_rows * width), preferred_element_type=F32
        )
        return made.astype(BF16).astype(F32).reshape(n_groups, per_group, rank_rows, width)

    made = jnp.stack([generate(head_a), generate(head_b)], 1)
    made = made.reshape(n_groups, 2 * per_group * rank_rows, width)
    made = exchange(made, "dp", n_groups, True, 1).astype(BF16)
    made = made.reshape(n_groups, 2, per_group, rank_rows, width)
    made = made.transpose(1, 2, 0, 3, 4).reshape(2, per_group, rank, width)
    down_weight, up_weight = made[0], made[1]
    full_a = exchange(down_weight.reshape(per_group * rank, width), "tensor", n_shards, False, 2).astype(BF16)
    full_a = jnp.swapaxes(full_a, 0, 1).reshape(per_group, rank, model_width)
    which = shard * rows_dev // block
    a_here = lax.dynamic_index_in_dim(full_a, which, 0, keepdims=False)

    grads_in = cotangent.reshape(per_group, block, width)
    back_part = jnp.einsum("gps,grs->pgr", up_weight, grads_in, preferred_element_type=F32)
    down_own = jnp.einsum("ps,rs->pr", a_here, tokens, preferred_element_type=F32)
    both_parts = jnp.concatenate([back_part.reshape(rank, rows_all), down_own], 1)
    both_parts = exchange(both_parts, "tensor", n_shards, False, 3)
    back_low = both_parts[:, :, :rows_all].sum(0).astype(BF16)
    down_low = jnp.swapaxes(both_parts[:, :, rows_all:], 0, 1).reshape(rank, rows_all).astype(BF16)

    base = jnp.dot(whole, w_query, preferred_element_type=F32)
    update = jnp.einsum(
        "pgr,gpn->grn",
        down_low.reshape(rank, per_group, block),
        up_weight,
        preferred_element_type=F32,
    ).reshape(rows_all, width)
    output = (base + update).astype(BF16)

    back_here = lax.dynamic_slice_in_dim(back_low, shard * rows_dev, rows_dev, 1)
    grad_tokens = (
        frozen
        + jnp.einsum("pr,pd->rd", back_here, a_here, preferred_element_type=F32)
    ).astype(BF16)

    scale = 1.0 / block
    columns = lax.dynamic_slice_in_dim(whole, shard * width, width, 1)
    grad_a = jnp.einsum(
        "pgr,grd->pgd",
        back_low.reshape(rank, per_group, block),
        columns.reshape(per_group, block, width),
        preferred_element_type=F32,
    )
    grad_b = jnp.einsum(
        "pgr,grd->pgd",
        down_low.reshape(rank, per_group, block),
        grads_in,
        preferred_element_type=F32,
    )

    low = (jnp.stack([grad_a, grad_b]) * scale).astype(BF16).astype(F32)
    low = jnp.swapaxes(low.reshape(2, n_groups, rank_rows * per_group, width), 0, 1)
    got = exchange(
        low.reshape(n_groups, 2 * rank_rows * per_group, width), "dp", n_groups, True, 4
    )
    got = got.reshape(n_groups, 2, rank_rows, per_group, width)
    got = got.transpose(1, 0, 3, 2, 4).reshape(2, blocks, rank_rows, width)

    hid_f = hidden.astype(F32)

    def head_grad(got):
        return sum(
            hid_f[b][:, None, None] * got[b][None] for b in range(blocks)
        ).astype(BF16)

    grad_head_b = head_grad(got[1])
    grad_head_a = head_grad(got[0])
    return (output, grad_tokens, grad_head_a, grad_head_b)


def solution(mesh):
    return jax.shard_map(
        local,
        mesh=mesh,
        in_specs=(
            P(("dp", "tensor"), None),
            P(None, "tensor"),
            P("dp", "tensor"),
            P(),
            P(None, "tensor"),
            P(None, "dp", "tensor"),
            P(None, "dp", "tensor"),
            P(),
        ),
        out_specs=(
            P("dp", "tensor"),
            P(("dp", "tensor"), None),
            P(None, "dp", "tensor"),
            P(None, "dp", "tensor"),
        ),
        check_vma=False,
    )
```

```python
import functools

import jax
import jax.numpy as jnp
from jax import lax
from jax.experimental import pallas as pl
from jax.experimental.pallas import tpu as pltpu
from jax.sharding import PartitionSpec as P

F32 = jnp.float32
BF16 = jnp.bfloat16
MESH = pl.DeviceIdType.MESH
GRAD_CHUNKS = 8
SKEW = 2


def exchange_kernel(axis, n, scatter, x_ref, out_ref, send_sem, recv_sem):
    me = lax.axis_index(axis)
    barrier = pltpu.get_barrier_semaphore()
    for k in range(1, n):
        pl.semaphore_signal(
            barrier, inc=1, device_id={axis: lax.rem(me + k, n)}, device_id_type=MESH
        )
    pl.semaphore_wait(barrier, n - 1)
    copies = []
    for k in range(1, n):
        target = lax.rem(me + k, n)
        copy = pltpu.make_async_remote_copy(
            src_ref=x_ref.at[target] if scatter else x_ref,
            dst_ref=out_ref.at[me],
            send_sem=send_sem.at[k],
            recv_sem=recv_sem.at[k],
            device_id={axis: target},
            device_id_type=MESH,
        )
        copy.start()
        copies.append(copy)
    out_ref[me] = x_ref[me] if scatter else x_ref[...]
    for copy in copies:
        copy.wait()


def exchange(x, axis, n, scatter, cid):
    rows, lanes = x.shape[-2:]
    x = x.astype(F32)
    x = jnp.pad(x, [(0, 0)] * (x.ndim - 2) + [(0, -rows % 8), (0, -lanes % 128)])
    shape = x.shape if scatter else (n,) + x.shape
    got = pl.pallas_call(
        functools.partial(exchange_kernel, axis, n, scatter),
        out_shape=jax.ShapeDtypeStruct(shape, x.dtype),
        in_specs=[pl.BlockSpec(memory_space=pltpu.VMEM)],
        out_specs=pl.BlockSpec(memory_space=pltpu.VMEM),
        scratch_shapes=[pltpu.SemaphoreType.DMA((n,)), pltpu.SemaphoreType.DMA((n,))],
        compiler_params=pltpu.CompilerParams(collective_id=cid, has_side_effects=True),
    )(x)
    return got[..., :rows, :lanes]


def gradient_kernel(n, chunks, g_ref, w_ref, out_ref, w_buf, mine, give, theirs, up_out, up_in, down_out, down_in,
                    w_sem, pair_send, pair_recv, up_send, up_recv, down_send, down_recv):
    shard = lax.axis_index("tensor")
    z, core = shard // 2, lax.rem(shard, 2)
    chips = n // 2
    steps = chips - 1
    rows = out_ref.shape[0]
    cw = w_buf.shape[1]
    pair = {"tensor": 2 * z + 1 - core}
    above = {"tensor": lax.rem(shard + 2, n)}
    below = {"tensor": lax.rem(shard + n - 2, n)}
    has_above, has_below = z < chips - 1, z > 0

    barrier = pltpu.get_barrier_semaphore()
    pl.semaphore_signal(barrier, inc=1, device_id=pair, device_id_type=MESH)

    @pl.when(has_above)
    def _():
        pl.semaphore_signal(barrier, inc=1, device_id=above, device_id_type=MESH)

    @pl.when(has_below)
    def _():
        pl.semaphore_signal(barrier, inc=1, device_id=below, device_id_type=MESH)

    def fetch(c):
        slot = lax.rem(c, 2)
        return pltpu.make_async_copy(
            w_ref.at[pl.ds(pl.multiple_of(c * cw, cw), cw)], w_buf.at[slot], w_sem.at[slot]
        )

    fetch(0).start()
    pl.semaphore_wait(
        barrier, 1 + jnp.where(has_above, 1, 0) + jnp.where(has_below, 1, 0)
    )

    def pair_copy(c):
        return pltpu.make_async_remote_copy(
            src_ref=give.at[c],
            dst_ref=theirs.at[c],
            send_sem=pair_send.at[c],
            recv_sem=pair_recv.at[c],
            device_id=pair,
            device_id_type=MESH,
        )

    def up_copy(c, s):
        return pltpu.make_async_remote_copy(
            src_ref=up_out.at[c, s],
            dst_ref=up_in.at[c, s],
            send_sem=up_send.at[c, s],
            recv_sem=up_recv.at[c, s],
            device_id=above,
            device_id_type=MESH,
        )

    def down_copy(c, s):
        return pltpu.make_async_remote_copy(
            src_ref=down_out.at[c, s],
            dst_ref=down_in.at[c, s],
            send_sem=down_send.at[c, s],
            recv_sem=down_recv.at[c, s],
            device_id=below,
            device_id_type=MESH,
        )

    def product(i, w):
        return lax.dot_general(
            g_ref[i], w, (((1,), (1,)), ((), ())), preferred_element_type=F32
        ).astype(BF16).reshape(chips, rows, cw)

    def multiply(c):
        @pl.when(c + 1 < chunks)
        def _():
            fetch(c + 1).start()

        fetch(c).wait()
        w = w_buf[lax.rem(c, 2)]
        give[c] = product(0, w)
        pair_copy(c).start()
        mine[c] = product(1, w)

    def both(c, d):
        return mine[c, d].astype(F32) + theirs[c, d].astype(F32)

    def forward(c, s):
        if s == 0:
            pair_copy(c).wait_recv()
        far = steps - s

        @pl.when(z <= s)
        def _():
            total = both(c, z + far)
            if s == 0:
                up_out[c, s] = total.astype(BF16)
            else:
                @pl.when(has_below)
                def _():
                    up_copy(c, s - 1).wait_recv()
                    up_out[c, s] = (total + up_in[c, s - 1].astype(F32)).astype(BF16)

                @pl.when(jnp.logical_not(has_below))
                def _():
                    up_out[c, s] = total.astype(BF16)
            up_copy(c, s).start()

        @pl.when(z >= far)
        def _():
            total = both(c, z - far)
            if s == 0:
                down_out[c, s] = total.astype(BF16)
            else:
                @pl.when(has_above)
                def _():
                    down_copy(c, s - 1).wait_recv()
                    down_out[c, s] = (total + down_in[c, s - 1].astype(F32)).astype(BF16)

                @pl.when(jnp.logical_not(has_above))
                def _():
                    down_out[c, s] = total.astype(BF16)
            down_copy(c, s).start()

    def finish(c):
        columns = pl.ds(pl.multiple_of(c * cw, cw), cw)
        if steps == 0:
            pair_copy(c).wait_recv()
        out_ref[:, columns] = both(c, z)
        if steps:
            @pl.when(has_below)
            def _():
                up_copy(c, steps - 1).wait_recv()
                out_ref[:, columns] += up_in[c, steps - 1].astype(F32)

            @pl.when(has_above)
            def _():
                down_copy(c, steps - 1).wait_recv()
                out_ref[:, columns] += down_in[c, steps - 1].astype(F32)

    def at(c, stage):
        @pl.when(jnp.logical_and(c >= 0, c < chunks))
        def _():
            stage(c)

    def turn(t, carry):
        at(t, multiply)
        for s in range(steps):
            at(t - 1 - SKEW * s, lambda c, s=s: forward(c, s))
        at(t - 1 - SKEW * steps, finish)
        return carry

    lax.fori_loop(0, chunks + 1 + SKEW * steps, turn, 0)

    def settle(c, carry):
        pair_copy(c).wait_send()
        for s in range(steps):
            @pl.when(z <= s)
            def _(s=s):
                up_copy(c, s).wait_send()

            @pl.when(z >= steps - s)
            def _(s=s):
                down_copy(c, s).wait_send()
        return carry

    lax.fori_loop(0, chunks, settle, 0)


def summed_gradient(grads, w, n, rows, cid):
    chips = n // 2
    model_width, width = w.shape
    cw = model_width // GRAD_CHUNKS
    steps = max(chips - 1, 1)
    all_rows = pltpu.VMEM((GRAD_CHUNKS, chips, rows, cw), BF16)
    hops = pltpu.VMEM((GRAD_CHUNKS, steps, rows, cw), BF16)
    pair_sem = pltpu.SemaphoreType.DMA((GRAD_CHUNKS,))
    hop_sem = pltpu.SemaphoreType.DMA((GRAD_CHUNKS, steps))
    vmem = pl.BlockSpec(memory_space=pltpu.VMEM)
    return pl.pallas_call(
        functools.partial(gradient_kernel, n, GRAD_CHUNKS),
        out_shape=jax.ShapeDtypeStruct((rows, model_width), F32),
        in_specs=[vmem, pl.BlockSpec(memory_space=pl.ANY)],
        out_specs=vmem,
        scratch_shapes=[pltpu.VMEM((2, cw, width), BF16)]
        + [all_rows] * 3
        + [hops] * 4
        + [pltpu.SemaphoreType.DMA((2,))]
        + [pair_sem] * 2
        + [hop_sem] * 4,
        compiler_params=pltpu.CompilerParams(
            collective_id=cid, has_side_effects=True, vmem_limit_bytes=48 * 1024 * 1024
        ),
        cost_estimate=pl.CostEstimate(
            flops=2 * rows * n * model_width * width,
            bytes_accessed=model_width * width * 12,
            transcendentals=0,
        ),
    )(grads, w)


def local(tokens, w_query, cotangent, task_embed, w_hidden, head_a, head_b, block_task):
    n_groups = lax.axis_size("dp")
    n_shards = lax.axis_size("tensor")
    chips = n_shards // 2
    shard = lax.axis_index("tensor")
    z, core = shard // 2, shard % 2
    hid_count, rank_rows, width = head_a.shape
    rank = rank_rows * n_groups
    blocks = block_task.shape[0]
    per_group = blocks // n_groups
    rows_dev, model_width = tokens.shape
    rows_all = rows_dev * n_shards
    block = rows_all // per_group

    whole = lax.all_gather(tokens, "tensor", axis=0, tiled=True)

    by_core = cotangent.reshape(chips, 2, rows_dev, width)
    by_core = jnp.where(core == 0, by_core[:, ::-1], by_core)
    by_core = jnp.swapaxes(by_core, 0, 1).reshape(2, chips * rows_dev, width)
    frozen = summed_gradient(by_core, w_query, n_shards, rows_dev, 6)

    part = jax.nn.silu(
        jnp.dot(task_embed[block_task], w_hidden, preferred_element_type=F32)
    ).astype(BF16)
    hidden = exchange(part.astype(F32), "tensor", n_shards, False, 0)
    hidden = jnp.swapaxes(hidden, 0, 1).reshape(blocks, hid_count).astype(BF16)

    def generate(head):
        made = jnp.dot(
            hidden, head.reshape(hid_count, rank_rows * width), preferred_element_type=F32
        )
        return made.astype(BF16).astype(F32).reshape(n_groups, per_group, rank_rows, width)

    made = jnp.stack([generate(head_a), generate(head_b)], 1)
    made = made.reshape(n_groups, 2 * per_group * rank_rows, width)
    made = exchange(made, "dp", n_groups, True, 1).astype(BF16)
    made = made.reshape(n_groups, 2, per_group, rank_rows, width)
    made = made.transpose(1, 2, 0, 3, 4).reshape(2, per_group, rank, width)
    down_weight, up_weight = made[0], made[1]
    full_a = exchange(down_weight.reshape(per_group * rank, width), "tensor", n_shards, False, 2).astype(BF16)
    full_a = jnp.swapaxes(full_a, 0, 1).reshape(per_group, rank, model_width)
    which = shard * rows_dev // block
    a_here = lax.dynamic_index_in_dim(full_a, which, 0, keepdims=False)

    grads_in = cotangent.reshape(per_group, block, width)
    back_part = jnp.einsum("gps,grs->pgr", up_weight, grads_in, preferred_element_type=F32)
    down_own = jnp.einsum("ps,rs->pr", a_here, tokens, preferred_element_type=F32)
    both_parts = jnp.concatenate([back_part.reshape(rank, rows_all), down_own], 1)
    both_parts = exchange(both_parts, "tensor", n_shards, False, 3)
    back_low = both_parts[:, :, :rows_all].sum(0).astype(BF16)
    down_low = jnp.swapaxes(both_parts[:, :, rows_all:], 0, 1).reshape(rank, rows_all).astype(BF16)

    base = jnp.dot(whole, w_query, preferred_element_type=F32)
    update = jnp.einsum(
        "pgr,gpn->grn",
        down_low.reshape(rank, per_group, block),
        up_weight,
        preferred_element_type=F32,
    ).reshape(rows_all, width)
    output = (base + update).astype(BF16)

    back_here = lax.dynamic_slice_in_dim(back_low, shard * rows_dev, rows_dev, 1)
    grad_tokens = (
        frozen
        + jnp.einsum("pr,pd->rd", back_here, a_here, preferred_element_type=F32)
    ).astype(BF16)

    scale = 1.0 / block
    columns = lax.dynamic_slice_in_dim(whole, shard * width, width, 1)
    grad_a = jnp.einsum(
        "pgr,grd->pgd",
        back_low.reshape(rank, per_group, block),
        columns.reshape(per_group, block, width),
        preferred_element_type=F32,
    )
    grad_b = jnp.einsum(
        "pgr,grd->pgd",
        down_low.reshape(rank, per_group, block),
        grads_in,
        preferred_element_type=F32,
    )

    low = (jnp.stack([grad_a, grad_b]) * scale).astype(BF16).astype(F32)
    low = jnp.swapaxes(low.reshape(2, n_groups, rank_rows * per_group, width), 0, 1)
    got = exchange(
        low.reshape(n_groups, 2 * rank_rows * per_group, width), "dp", n_groups, True, 4
    )
    got = got.reshape(n_groups, 2, rank_rows, per_group, width)
    got = got.transpose(1, 0, 3, 2, 4).reshape(2, blocks, rank_rows, width)

    hid_f = hidden.astype(F32)

    def head_grad(got):
        return sum(
            hid_f[b][:, None, None] * got[b][None] for b in range(blocks)
        ).astype(BF16)

    grad_head_b = head_grad(got[1])
    grad_head_a = head_grad(got[0])
    return (output, grad_tokens, grad_head_a, grad_head_b)


def solution(mesh):
    return jax.shard_map(
        local,
        mesh=mesh,
        in_specs=(
            P(("dp", "tensor"), None),
            P(None, "tensor"),
            P("dp", "tensor"),
            P(),
            P(None, "tensor"),
            P(None, "dp", "tensor"),
            P(None, "dp", "tensor"),
            P(),
        ),
        out_specs=(
            P("dp", "tensor"),
            P(("dp", "tensor"), None),
            P(None, "dp", "tensor"),
            P(None, "dp", "tensor"),
        ),
        check_vma=False,
    )
```
